128 devices in a mesh: row: 8 (over y_hi, x), col: 16 (over y_lo, z, core).
Axes of the slice: x: 4, y: 4 (y_hi: 2, y_lo: 2; y = y_hi * 2 + y_lo), z: 4, core: 2. Of those that a mesh axis runs over, the one named last changes fastest.
Arguments:
- replay_pool: bfloat16 [8192, 512], P('row'), may hold values from -6 to 6
- sample_ids: int32 [8, 1024], P('row'), may hold values from 0 to 1023, each once within a row
- rotation_bins: int32 [8192], P('row'), may hold values from 0 to 15
Outputs:
- factored: float32 [8192, 8192], P('row', 'col')
The draws below stay inside these ranges and needn't reach their ends.
Inputs may be any that keep to these rules, and one draw needn't show every extreme that they name: Each row of sample_ids is a permutation of 0 to 1023.
All inputs are finite; a program needn't handle non-finite values.
Results may differ from the reference program's by a relative error of at most 0.0003.
Values may be sent and summed in bfloat16 or wider, within the bound.
A program may use at most 128 MiB of HBM per device.

```python
import jax
import jax.numpy as jnp
from jax import lax

F = 512
ROTS = 16
ROWS_DEV = 1024
CHANNELS = 32
ROWGRID = 8
COLGRID = 16
N = 8192
NB_R = 128
NB_C = 64
PANEL = 1024


latent_rank = 8


noise_level = 0.5


def draw_replay_pool(key, part):
    keys = jax.random.split(jax.random.fold_in(key, 7), 5)
    latent = jax.random.normal(keys[0], (N, latent_rank), jnp.float32)
    noise = jax.random.normal(keys[1], (N, F), jnp.float32)
    amplitude = jax.random.normal(keys[3], (latent_rank, 1, CHANNELS), jnp.float32)
    phase = jax.random.uniform(keys[4], (latent_rank, 1, CHANNELS), jnp.float32, 0.0, 2.0 * jnp.pi)
    bins = jnp.arange(ROTS, dtype=jnp.float32)[None, :, None]
    freqs = jnp.arange(latent_rank, dtype=jnp.float32)[:, None, None]
    pattern = 1.4142135 * amplitude * jnp.cos(2.0 * jnp.pi * freqs * bins / ROTS + phase)
    pattern = pattern.reshape(latent_rank, F)
    signal = jnp.zeros((N, F), jnp.float32)
    for factor in range(latent_rank):
        signal = signal + latent[:, factor:factor + 1] * pattern[factor][None, :]
    signal = signal / jnp.sqrt(jnp.float32(latent_rank))
    values = signal + noise_level * noise
    return jnp.clip(values, -6.0, 6.0).astype(jnp.bfloat16)


def plant(values, rng, smallest, high):
    spot = [jax.random.randint(jax.random.fold_in(rng, axis), (), 0, length) for axis, length in enumerate(values.shape)]
    main_axis = values.shape.index(max(values.shape))
    neighbour = spot[:main_axis] + [(spot[main_axis] + 1) % values.shape[main_axis]] + spot[main_axis + 1:]
    return values.at[tuple(spot)].set(smallest).at[tuple(neighbour)].set(high)


def setup_inputs(seed: int = 0) -> dict:
    key_list = jax.random.split(jax.random.key(seed), 4)
    return {
        "replay_pool": draw_replay_pool(jax.random.fold_in(key_list[3], 71), 0),
        "sample_ids": jax.vmap(lambda own: jax.random.permutation(own, ROWS_DEV))(jax.random.split(key_list[1], ROWGRID)).reshape((ROWGRID, ROWS_DEV)).astype(jnp.int32),
        "rotation_bins": plant(jax.random.randint(key_list[2], (N,), 0, ROTS), jax.random.fold_in(key_list[2], 1), 0, ROTS - 1).astype(jnp.int32),
    }


sharpness = 2.0
ridge_weight = 0.1
highest = lax.Precision.HIGHEST

def action_weight(row_rot, col_rot):
    bin_gap = (row_rot[:, None] - col_rot[None, :]).astype(jnp.float32)
    return jnp.exp(sharpness * (jnp.cos(bin_gap * (2.0 * jnp.pi / ROTS)) - 1.0))

def orbit_kernel(row_feats, row_rot, col_feats, col_rot):
    rows_wide = row_feats.astype(jnp.float32)
    cols_wide = col_feats.astype(jnp.float32)
    row_norms = jnp.sum(rows_wide * rows_wide, axis=1)
    col_norms = jnp.sum(cols_wide * cols_wide, axis=1)
    col_binned = cols_wide.reshape(cols_wide.shape[0], ROTS, CHANNELS)

    def one_rotation(summed, rotation):
        rolled = jnp.roll(col_binned, rotation, axis=1).reshape(cols_wide.shape[0], F)
        products = jnp.dot(rows_wide, rolled.T, precision=highest)
        distance = row_norms[:, None] + col_norms[None, :] - 2.0 * products
        return (summed + jnp.exp(-distance / F), None)
    start = jnp.zeros((rows_wide.shape[0], cols_wide.shape[0]), jnp.float32)
    summed, _ = lax.scan(one_rotation, start, jnp.arange(ROTS, dtype=jnp.int32))
    return action_weight(row_rot, col_rot) * summed / ROTS

def reference(replay_pool, sample_ids, rotation_bins):
    offsets = (jnp.arange(ROWGRID, dtype=jnp.int32) * ROWS_DEV)[:, None]
    features = replay_pool[(sample_ids + offsets).reshape(N)]
    kernel_full = orbit_kernel(features, rotation_bins, features, rotation_bins)
    kernel_full = kernel_full + ridge_weight * jnp.eye(N, dtype=jnp.float32)
    diag_factor = jnp.linalg.cholesky(kernel_full[:PANEL, :PANEL])
    panel = jax.scipy.linalg.solve_triangular(diag_factor, kernel_full[:, :PANEL].T, lower=True).T
    trailing = kernel_full[:, PANEL:] - jnp.dot(panel, panel[PANEL:].T, precision=highest)
    updated = jnp.concatenate([panel, trailing], axis=1)
    by_rows = updated.reshape(ROWGRID, ROWGRID, NB_R, N).transpose(1, 0, 2, 3).reshape(N, N)
    return by_rows.reshape(N, ROWGRID, COLGRID, NB_C).transpose(0, 2, 1, 3).reshape(N, N)
```

```python
import functools
import math

import jax
import jax.numpy as jnp
import numpy as np
from jax import lax
from jax.experimental import pallas as pl
from jax.experimental.pallas import tpu as pltpu
from jax.sharding import PartitionSpec as P

MESH = pl.DeviceIdType.MESH
f32 = jnp.float32
bf16 = jnp.bfloat16

ROTS = 16
SHARPNESS = 2.0
RIDGE = 0.1
F = 512
E = 640
G = 8
Q = 16
LOG2E = math.log2(math.e)
SCALE = 2.0 * LOG2E / F
VMEM = pl.BlockSpec(memory_space=pltpu.VMEM)
ROOM = 56 * 2**20


def split3(x):
    a = x.astype(bf16)
    x = x - a.astype(f32)
    b = x.astype(bf16)
    return a, b, (x - b.astype(f32)).astype(bf16)


def split(x):
    hi = x.astype(bf16)
    return hi, (x - hi.astype(f32)).astype(bf16)


def dot(a, b, dims):
    return lax.dot_general(a, b, (dims, ((), ())), preferred_element_type=f32)


def dot3(a, b, dims):
    ah, al = a
    bh, bl = b
    return dot(ah, bh, dims) + (dot(ah, bl, dims) + dot(al, bh, dims))


NT = ((1,), (1,))
NN = ((1,), (0,))
TN = ((0,), (0,))


def bin_table():
    angle = 2.0 * np.pi * np.arange(ROTS) / ROTS
    table = np.zeros((128, 128), np.float64)
    root = math.sqrt(SHARPNESS * LOG2E)
    for first, values in ((6, root * np.cos(angle)), (12, root * np.sin(angle))):
        parts, rest = [], values
        for _ in range(3):
            part = rest.astype(np.float32).astype(jnp.bfloat16).astype(np.float64)
            parts.append(part)
            rest = rest - part
        for lane, (left, right) in enumerate(((0, 0), (0, 1), (1, 0), (0, 2), (1, 1), (2, 0))):
            table[:ROTS, first + lane] = parts[left]
            table[:ROTS, 64 + first + lane] = parts[right]
    table[:ROTS, 3:6] = 1.0
    table[:ROTS, 64:67] = 1.0
    return table.astype(np.float32).astype(jnp.bfloat16)


def prep_kernel(pool_ref, ids_ref, rot_ref, table_ref, out_ref):
    def chunk(i, _):
        o = pl.multiple_of(i * 256, 256)
        n = pool_ref.shape[0]
        pick = lax.broadcasted_iota(jnp.int32, (256, n), 1) == ids_ref[pl.ds(o, 256), :]
        feats = dot(jnp.where(pick, 1.0, 0.0).astype(bf16), pool_ref[...], NN)
        norm = jnp.sum(feats * feats, axis=1, keepdims=True)
        a = jnp.broadcast_to(norm * (-LOG2E / F) - (SHARPNESS * LOG2E / 2.0 + 2.0), (256, 128))
        lane = lax.broadcasted_iota(jnp.int32, (256, 128), 1)
        bins = jnp.where(lane == rot_ref[pl.ds(o, 256), :], 1.0, 0.0).astype(bf16)
        extra = dot(bins, table_ref[...], NN)
        for k, part in enumerate(split3(a)):
            extra = jnp.where((lane == k) | (lane == 64 + 3 + k), part.astype(f32), extra)
        out_ref[pl.ds(o, 256), :F] = feats.astype(bf16)
        out_ref[pl.ds(o, 256), F:] = extra.astype(bf16)
        return 0

    lax.fori_loop(0, pool_ref.shape[0] // 256, chunk, 0)


def prep(pool, ids, rot):
    n = pool.shape[0]
    return pl.pallas_call(
        prep_kernel,
        out_shape=jax.ShapeDtypeStruct((n, E), bf16),
        in_specs=[VMEM] * 4,
        out_specs=VMEM,
        compiler_params=pltpu.CompilerParams(vmem_limit_bytes=ROOM),
    )(pool, ids.reshape(n, 1), rot.reshape(n, 1), jnp.asarray(bin_table()))


def exchange_kernel(ext_ref, rows_ref, cols_ref, lead_ref, local, s_row, r_row, s_col, r_col, s_lead, r_lead):
    p = lax.axis_index("row")
    q = lax.axis_index("col")
    barrier = pltpu.get_barrier_semaphore()
    for d in range(1, G):
        pl.semaphore_signal(barrier, inc=1, device_id=(lax.rem(p + d, G), q), device_id_type=MESH)
    for d in range(1, Q):
        pl.semaphore_signal(barrier, inc=1, device_id=(p, lax.rem(q + d, Q)), device_id_type=MESH)
    pl.semaphore_wait(barrier, G - 1 + Q - 1)

    def mine(k, width):
        return pl.ds(pl.multiple_of(k * width, width), width)

    def col_copy(d):
        return pltpu.make_async_remote_copy(
            src_ref=ext_ref.at[mine(q, 64), :],
            dst_ref=cols_ref.at[mine(p, 64), :],
            send_sem=s_col.at[d - 1], recv_sem=r_col.at[p],
            device_id=(lax.rem(p + d, G), q), device_id_type=MESH)

    def row_copy(d):
        other = lax.rem(p + d, G)
        return pltpu.make_async_remote_copy(
            src_ref=ext_ref.at[mine(other, 128), :],
            dst_ref=rows_ref.at[mine(p, 128), :],
            send_sem=s_row.at[d - 1], recv_sem=r_row.at[p],
            device_id=(other, q), device_id_type=MESH)

    def lead_copy(d):
        return pltpu.make_async_remote_copy(
            src_ref=cols_ref.at[pl.ds(0, 64), :],
            dst_ref=lead_ref.at[mine(q, 64), :],
            send_sem=s_lead.at[d - 1], recv_sem=r_lead.at[q],
            device_id=(p, lax.rem(q + d, Q)), device_id_type=MESH)

    def landed(ref, k, width, sem):
        return pltpu.make_async_remote_copy(
            src_ref=ref.at[mine(k, width), :], dst_ref=ref.at[mine(k, width), :],
            send_sem=s_row.at[0], recv_sem=sem.at[k],
            device_id=(lax.rem(p + 1, G), q), device_id_type=MESH)

    own_col = pltpu.make_async_copy(ext_ref.at[mine(q, 64), :], cols_ref.at[mine(p, 64), :], local.at[0])
    own_row = pltpu.make_async_copy(ext_ref.at[mine(p, 128), :], rows_ref.at[mine(p, 128), :], local.at[1])
    own_col.start()
    cols = [col_copy(d) for d in range(1, G)]
    for c in cols:
        c.start()
    own_row.start()
    own_col.wait()

    @pl.when(p != 0)
    def _():
        landed(cols_ref, 0, 64, r_col).wait_recv()

    own_lead = pltpu.make_async_copy(cols_ref.at[pl.ds(0, 64), :], lead_ref.at[mine(q, 64), :], local.at[2])
    own_lead.start()
    leads = [lead_copy(d) for d in range(1, Q)]
    for c in leads:
        c.start()
    rows = [row_copy(d) for d in range(1, G)]
    for c in rows:
        c.start()
    own_row.wait()
    own_lead.wait()
    for c in cols + leads + rows:
        c.wait_send()
    for k in range(1, G):
        @pl.when(p != k)
        def _():
            landed(cols_ref, k, 64, r_col).wait_recv()
    for k in range(Q):
        @pl.when(q != k)
        def _():
            landed(lead_ref, k, 64, r_lead).wait_recv()
    for k in range(G):
        @pl.when(p != k)
        def _():
            landed(rows_ref, k, 128, r_row).wait_recv()


def exchange(ext):
    n = ext.shape[0]
    dma = pltpu.SemaphoreType.DMA
    return pl.pallas_call(
        exchange_kernel,
        out_shape=(jax.ShapeDtypeStruct((n, E), bf16), jax.ShapeDtypeStruct((n // 2, E), bf16),
                   jax.ShapeDtypeStruct((n, E), bf16)),
        in_specs=[VMEM],
        out_specs=(VMEM,) * 3,
        scratch_shapes=[dma((3,)), dma((G - 1,)), dma((G,)), dma((G - 1,)), dma((G,)), dma((Q - 1,)), dma((Q,))],
        compiler_params=pltpu.CompilerParams(collective_id=0, has_side_effects=True, vmem_limit_bytes=ROOM),
    )(ext)


def turned(cols_ref, o, r4, aux):
    feats = cols_ref[pl.ds(o, 256), :F].astype(f32)
    for r in range(4):
        r4[r] = (jnp.roll(feats, 32 * r, axis=1) if r else feats).astype(bf16)
    aux[...] = jnp.roll(cols_ref[pl.ds(o, 256), F:].astype(f32), 64, axis=1).astype(bf16)


def tile(rows, r4, aux):
    lane = lax.broadcasted_iota(jnp.int32, (rows.shape[0], 128), 1)
    left = jnp.where(lane < 64, rows[:, F:].astype(f32), 0.0).astype(bf16)
    lhs = rows[:, :F]
    total = None
    for r in range(4):
        x = r4[r]
        for h in range(4):
            w = jnp.concatenate([x[:, 128 * ((k - h) % 4):128 * ((k - h) % 4) + 128] for k in range(4)], axis=1)
            e = jnp.exp2(dot(lhs, w, NT) * SCALE)
            total = e if total is None else total + e
    return total * jnp.exp2(dot(left, aux[...], NT))


def kernel_kernel(rows_ref, cols_ref, lead_ref, krh, krl, kch, kcl, ktr, lead_k, r4, aux):
    p = lax.axis_index("row")
    q = lax.axis_index("col")
    tm = 512

    def iotas(m, o, oc):
        return (o + lax.broadcasted_iota(jnp.int32, (m, 256), 0), oc + lax.broadcasted_iota(jnp.int32, (m, 256), 1))

    def lead_tile(n, _):
        oc = pl.multiple_of(n * 256, 256)
        turned(lead_ref, oc, r4, aux)

        def own(m, _):
            o = pl.multiple_of(m * 256, 256)
            k = tile(lead_ref[pl.ds(o, 256), :], r4, aux)
            i, j = iotas(256, o, oc)
            lead_k[pl.ds(o, 256), pl.ds(oc, 256)] = k + jnp.where(i == j, RIDGE, 0.0)
            return 0

        lax.fori_loop(0, n + 1, own, 0)

        def rows(m, _):
            o = pl.multiple_of(m * tm, tm)
            k = tile(rows_ref[pl.ds(o, tm), :], r4, aux)
            i, j = iotas(tm, o, oc)
            k = k + jnp.where((i < 128) & (i + p * 128 == j), RIDGE, 0.0)
            krh[pl.ds(o, tm), pl.ds(oc, 256)], krl[pl.ds(o, tm), pl.ds(oc, 256)] = split(k)
            return 0

        lax.fori_loop(0, rows_ref.shape[0] // tm, rows, 0)
        k = tile(cols_ref[...], r4, aux)
        kch[:, pl.ds(oc, 256)], kcl[:, pl.ds(oc, 256)] = split(k)
        return 0

    lax.fori_loop(0, lead_ref.shape[0] // 256, lead_tile, 0)

    def tr_tile(n, _):
        oc = pl.multiple_of(n * 256, 256)
        turned(cols_ref, oc, r4, aux)

        def rows(m, _):
            o = pl.multiple_of(m * tm, tm)
            k = tile(rows_ref[pl.ds(o, tm), :], r4, aux)
            i, j = iotas(tm, o, oc)
            same = ((i >> 7) == (j >> 6)) & (p * 128 + (i & 127) == q * 64 + (j & 63))
            k = k + jnp.where(same, RIDGE, 0.0)
            ktr[pl.ds(o, tm), pl.ds(oc, 256)] = jnp.where(j < 64, 0.0, k)
            return 0

        lax.fori_loop(0, rows_ref.shape[0] // tm, rows, 0)
        return 0

    lax.fori_loop(0, cols_ref.shape[0] // 256, tr_tile, 0)


def kernels(rows, cols, lead):
    n, c, w = rows.shape[0], cols.shape[0], lead.shape[0]
    s = jax.ShapeDtypeStruct
    return pl.pallas_call(
        kernel_kernel,
        out_shape=(s((n, w), bf16), s((n, w), bf16), s((c, w), bf16), s((c, w), bf16), s((n, c), f32), s((w, w), f32)),
        in_specs=[VMEM] * 3,
        out_specs=(VMEM,) * 6,
        scratch_shapes=[pltpu.VMEM((4, 256, F), bf16), pltpu.VMEM((256, 128), bf16)],
        compiler_params=pltpu.CompilerParams(vmem_limit_bytes=ROOM),
    )(rows, cols, lead)


def factor_block(S,V):
    sub=lax.broadcasted_iota(jnp.int32,(8,128),0)
    out=[]
    for b in range(16):
        R=S[b]; W=V[b]
        B=[jnp.broadcast_to(R[:,8*b+k:8*b+k+1],(8,128)) for k in range(8)]
        X=jnp.zeros((8,128),f32)
        for k in range(8):
            piv=jnp.broadcast_to(B[k][k:k+1,:],(8,128))
            rp=1.0/piv
            rs=lax.rsqrt(piv)
            here=sub==k
            mul=B[k]
            def step(Y):
                row=jnp.broadcast_to(Y[k:k+1,:],(8,128))*rp
                return jnp.where(here,row,Y-mul*row)
            X=jnp.where(here,W*rs,X)
            R=step(R); W=step(W)
            for j in range(k+1,8):
                B[j]=step(B[j])
        out.append(X)
        Rk=[jnp.broadcast_to(R[k:k+1,:],(8,128)) for k in range(8)]
        Wk=[jnp.broadcast_to(W[k:k+1,:],(8,128)) for k in range(8)]
        for r in range(b+1,16):
            c=[jnp.broadcast_to(S[r][:,8*b+k:8*b+k+1],(8,128)) for k in range(8)]
            S[r]=S[r]-(((c[0]*Rk[0]+c[1]*Rk[1])+(c[2]*Rk[2]+c[3]*Rk[3]))+((c[4]*Rk[4]+c[5]*Rk[5])+(c[6]*Rk[6]+c[7]*Rk[7])))
            V[r]=V[r]-(((c[0]*Wk[0]+c[1]*Wk[1])+(c[2]*Wk[2]+c[3]*Wk[3]))+((c[4]*Wk[4]+c[5]*Wk[5])+(c[6]*Wk[6]+c[7]*Wk[7])))
    return out

def chol_kernel(n, a_ref, x_ref, ph, plo):
    nb=n//128
    x_ref[...]=a_ref[...]
    ri=lax.broadcasted_iota(jnp.int32,(128,128),0); ci=lax.broadcasted_iota(jnp.int32,(128,128),1)
    eye=jnp.where(ri==ci,1.0,0.0).astype(f32)
    def outer(j,_):
        o=pl.multiple_of(j*128,128)
        D=x_ref[pl.ds(o,128),pl.ds(o,128)]
        S=[D[8*b:8*b+8] for b in range(16)]
        V=[eye[8*b:8*b+8] for b in range(16)]
        rows=factor_block(S,V)
        X=jnp.concatenate(rows,axis=0)
        x_ref[pl.ds(o,128),pl.ds(o,128)]=eye
        Xs=split(X)
        P=dot3(Xs,split(x_ref[pl.ds(o,128),:]),NN)
        x_ref[pl.ds(o,128),:]=P
        h,l=split(P)
        ph[...]=h; plo[...]=l
        def upd(i,_):
            oi=pl.multiple_of(i*128,128)
            F=(ph[:,pl.ds(oi,128)],plo[:,pl.ds(oi,128)])
            x_ref[pl.ds(oi,128),pl.ds(o,128)]=jnp.zeros((128,128),f32)
            x_ref[pl.ds(oi,128),:]=x_ref[pl.ds(oi,128),:]-dot3(F,(ph[...],plo[...]),TN)
            return 0
        lax.fori_loop(j+1,nb,upd,0)
        return 0
    lax.fori_loop(0,nb,outer,0)
    for j in range(nb-1):
        x_ref[j*128:(j+1)*128,(j+1)*128:]=jnp.zeros((128,n-(j+1)*128),f32)


def chol_inv(a):
    n = a.shape[0]
    return pl.pallas_call(
        functools.partial(chol_kernel, n),
        out_shape=jax.ShapeDtypeStruct((n, n), f32),
        in_specs=[VMEM],
        out_specs=VMEM,
        scratch_shapes=[pltpu.VMEM((128, n), bf16), pltpu.VMEM((128, n), bf16)],
        compiler_params=pltpu.CompilerParams(vmem_limit_bytes=ROOM),
    )(a)


def tail_kernel(krh, krl, kch, kcl, ktr, x_ref, out, xh, xl, ph, plo, zh, zl):
    q = lax.axis_index("col")
    n = x_ref.shape[0]
    for j in range(0, n, 256):
        xh[j:j + 256, :], xl[j:j + 256, :] = split(x_ref[j:j + 256, :])

    def cols(m, _):
        o = pl.ds(pl.multiple_of(m * 256, 256), 256)
        for j in range(0, n, 256):
            w = j + 256
            v = dot3((kch[o, :w], kcl[o, :w]), (xh[j:w, :w], xl[j:w, :w]), NT)
            ph[o, j:w], plo[o, j:w] = split(v)
        for j in range(0, n, 256):
            w = j + 256
            v = dot3((ph[o, j:], plo[o, j:]), (xh[j:, j:w], xl[j:, j:w]), NN)
            zh[o, j:w], zl[o, j:w] = split(v)
        return 0

    lax.fori_loop(0, kch.shape[0] // 256, cols, 0)
    first = pl.ds(pl.multiple_of(q * 64, 64), 64)
    zh[:64, :] = -xh[first, :]
    zl[:64, :] = -xl[first, :]

    def rows(m, _):
        o = pl.ds(pl.multiple_of(m * 256, 256), 256)
        out[o, :] = ktr[o, :] - dot3((krh[o, :], krl[o, :]), (zh[...], zl[...]), NT)
        return 0

    lax.fori_loop(0, krh.shape[0] // 256, rows, 0)


def tail(krh, krl, kch, kcl, ktr, x):
    n, w = krh.shape
    c = kch.shape[0]
    v = pltpu.VMEM
    return pl.pallas_call(
        tail_kernel,
        out_shape=jax.ShapeDtypeStruct((n, c), f32),
        in_specs=[VMEM] * 6,
        out_specs=VMEM,
        scratch_shapes=[v((w, w), bf16), v((w, w), bf16), v((c, w), bf16), v((c, w), bf16), v((c, w), bf16), v((c, w), bf16)],
        compiler_params=pltpu.CompilerParams(vmem_limit_bytes=ROOM),
    )(krh, krl, kch, kcl, ktr, x)


def per_device(pool, ids, rot):
    ext = prep(pool, ids, rot)
    rows, cols, lead = exchange(ext)
    krh, krl, kch, kcl, ktr, lead_k = kernels(rows, cols, lead)
    return tail(krh, krl, kch, kcl, ktr, chol_inv(lead_k))


def solution(mesh):
    return jax.shard_map(
        per_device,
        mesh=mesh,
        in_specs=(P("row", None), P("row", None), P("row")),
        out_specs=P("row", "col"),
        check_vma=False,
    )
```

```python
import functools
import math

import jax
import jax.numpy as jnp
import numpy as np
from jax import lax
from jax.experimental import pallas as pl
from jax.experimental.pallas import tpu as pltpu
from jax.sharding import PartitionSpec as P

MESH = pl.DeviceIdType.MESH
f32 = jnp.float32
bf16 = jnp.bfloat16

ROTS = 16
SHARPNESS = 2.0
RIDGE = 0.1
F = 512
E = 640
G = 8
Q = 16
LOG2E = math.log2(math.e)
SCALE = 2.0 * LOG2E / F
VMEM = pl.BlockSpec(memory_space=pltpu.VMEM)
ROOM = 56 * 2**20


def split3(x):
    a = x.astype(bf16)
    x = x - a.astype(f32)
    b = x.astype(bf16)
    return a, b, (x - b.astype(f32)).astype(bf16)


def split(x):
    hi = x.astype(bf16)
    return hi, (x - hi.astype(f32)).astype(bf16)


def dot(a, b, dims):
    return lax.dot_general(a, b, (dims, ((), ())), preferred_element_type=f32)


def dot3(a, b, dims):
    ah, al = a
    bh, bl = b
    return dot(ah, bh, dims) + (dot(ah, bl, dims) + dot(al, bh, dims))


NT = ((1,), (1,))
NN = ((1,), (0,))
TN = ((0,), (0,))


def bin_table():
    angle = 2.0 * np.pi * np.arange(ROTS) / ROTS
    table = np.zeros((128, 128), np.float64)
    root = math.sqrt(SHARPNESS * LOG2E)
    for first, values in ((6, root * np.cos(angle)), (12, root * np.sin(angle))):
        parts, rest = [], values
        for _ in range(3):
            part = rest.astype(np.float32).astype(jnp.bfloat16).astype(np.float64)
            parts.append(part)
            rest = rest - part
        for lane, (left, right) in enumerate(((0, 0), (0, 1), (1, 0), (0, 2), (1, 1), (2, 0))):
            table[:ROTS, first + lane] = parts[left]
            table[:ROTS, 64 + first + lane] = parts[right]
    table[:ROTS, 3:6] = 1.0
    table[:ROTS, 64:67] = 1.0
    return table.astype(np.float32).astype(jnp.bfloat16)


def prep_kernel(pool_ref, ids_ref, rot_ref, table_ref, out_ref):
    def chunk(i, _):
        o = pl.multiple_of(i * 256, 256)
        n = pool_ref.shape[0]
        pick = lax.broadcasted_iota(jnp.int32, (256, n), 1) == ids_ref[pl.ds(o, 256), :]
        feats = dot(jnp.where(pick, 1.0, 0.0).astype(bf16), pool_ref[...], NN)
        norm = jnp.sum(feats * feats, axis=1, keepdims=True)
        a = jnp.broadcast_to(norm * (-LOG2E / F) - (SHARPNESS * LOG2E / 2.0 + 2.0), (256, 128))
        lane = lax.broadcasted_iota(jnp.int32, (256, 128), 1)
        bins = jnp.where(lane == rot_ref[pl.ds(o, 256), :], 1.0, 0.0).astype(bf16)
        extra = dot(bins, table_ref[...], NN)
        for k, part in enumerate(split3(a)):
            extra = jnp.where((lane == k) | (lane == 64 + 3 + k), part.astype(f32), extra)
        out_ref[pl.ds(o, 256), :F] = feats.astype(bf16)
        out_ref[pl.ds(o, 256), F:] = extra.astype(bf16)
        return 0

    lax.fori_loop(0, pool_ref.shape[0] // 256, chunk, 0)


def prep(pool, ids, rot):
    n = pool.shape[0]
    return pl.pallas_call(
        prep_kernel,
        out_shape=jax.ShapeDtypeStruct((n, E), bf16),
        in_specs=[VMEM] * 4,
        out_specs=VMEM,
        compiler_params=pltpu.CompilerParams(vmem_limit_bytes=ROOM),
    )(pool, ids.reshape(n, 1), rot.reshape(n, 1), jnp.asarray(bin_table()))


def exchange_kernel(ext_ref, rows_ref, cols_ref, lead_ref, local, s_row, r_row, s_col, r_col, s_lead, r_lead):
    p = lax.axis_index("row")
    q = lax.axis_index("col")
    barrier = pltpu.get_barrier_semaphore()
    for d in range(1, G):
        pl.semaphore_signal(barrier, inc=1, device_id=(lax.rem(p + d, G), q), device_id_type=MESH)
    for d in range(1, Q):
        pl.semaphore_signal(barrier, inc=1, device_id=(p, lax.rem(q + d, Q)), device_id_type=MESH)
    pl.semaphore_wait(barrier, G - 1 + Q - 1)

    def mine(k, width):
        return pl.ds(pl.multiple_of(k * width, width), width)

    def col_copy(d):
        return pltpu.make_async_remote_copy(
            src_ref=ext_ref.at[mine(q, 64), :],
            dst_ref=cols_ref.at[mine(p, 64), :],
            send_sem=s_col.at[d - 1], recv_sem=r_col.at[p],
            device_id=(lax.rem(p + d, G), q), device_id_type=MESH)

    def row_copy(d):
        other = lax.rem(p + d, G)
        return pltpu.make_async_remote_copy(
            src_ref=ext_ref.at[mine(other, 128), :],
            dst_ref=rows_ref.at[mine(p, 128), :],
            send_sem=s_row.at[d - 1], recv_sem=r_row.at[p],
            device_id=(other, q), device_id_type=MESH)

    def lead_copy(d):
        return pltpu.make_async_remote_copy(
            src_ref=cols_ref.at[pl.ds(0, 64), :],
            dst_ref=lead_ref.at[mine(q, 64), :],
            send_sem=s_lead.at[d - 1], recv_sem=r_lead.at[q],
            device_id=(p, lax.rem(q + d, Q)), device_id_type=MESH)

    def landed(ref, k, width, sem):
        return pltpu.make_async_remote_copy(
            src_ref=ref.at[mine(k, width), :], dst_ref=ref.at[mine(k, width), :],
            send_sem=s_row.at[0], recv_sem=sem.at[k],
            device_id=(lax.rem(p + 1, G), q), device_id_type=MESH)

    own_col = pltpu.make_async_copy(ext_ref.at[mine(q, 64), :], cols_ref.at[mine(p, 64), :], local.at[0])
    own_row = pltpu.make_async_copy(ext_ref.at[mine(p, 128), :], rows_ref.at[mine(p, 128), :], local.at[1])
    own_col.start()
    cols = [col_copy(d) for d in range(1, G)]
    for c in cols:
        c.start()
    own_row.start()
    own_col.wait()

    @pl.when(p != 0)
    def _():
        landed(cols_ref, 0, 64, r_col).wait_recv()

    own_lead = pltpu.make_async_copy(cols_ref.at[pl.ds(0, 64), :], lead_ref.at[mine(q, 64), :], local.at[2])
    own_lead.start()
    leads = [lead_copy(d) for d in range(1, Q)]
    for c in leads:
        c.start()
    rows = [row_copy(d) for d in range(1, G)]
    for c in rows:
        c.start()
    own_row.wait()
    own_lead.wait()
    for c in cols + leads + rows:
        c.wait_send()
    for k in range(1, G):
        @pl.when(p != k)
        def _():
            landed(cols_ref, k, 64, r_col).wait_recv()
    for k in range(Q):
        @pl.when(q != k)
        def _():
            landed(lead_ref, k, 64, r_lead).wait_recv()
    for k in range(G):
        @pl.when(p != k)
        def _():
            landed(rows_ref, k, 128, r_row).wait_recv()


def exchange(ext):
    n = ext.shape[0]
    dma = pltpu.SemaphoreType.DMA
    return pl.pallas_call(
        exchange_kernel,
        out_shape=(jax.ShapeDtypeStruct((n, E), bf16), jax.ShapeDtypeStruct((n // 2, E), bf16),
                   jax.ShapeDtypeStruct((n, E), bf16)),
        in_specs=[VMEM],
        out_specs=(VMEM,) * 3,
        scratch_shapes=[dma((3,)), dma((G - 1,)), dma((G,)), dma((G - 1,)), dma((G,)), dma((Q - 1,)), dma((Q,))],
        compiler_params=pltpu.CompilerParams(collective_id=0, has_side_effects=True, vmem_limit_bytes=ROOM),
    )(ext)


def roll_into(src, o, r4):
    feats = src[pl.ds(o, 256), :F].astype(f32)
    for r in range(4):
        r4[r, pl.ds(o, 256), :] = (jnp.roll(feats, 32 * r, axis=1) if r else feats).astype(bf16)


def tile(rows, rolled, right):
    lane = lax.broadcasted_iota(jnp.int32, (rows.shape[0], 128), 1)
    left = jnp.where(lane < 64, rows[:, F:].astype(f32), 0.0).astype(bf16)
    lhs = rows[:, :F]
    total = None
    for r in range(4):
        x = rolled(r)
        for h in range(4):
            w = jnp.concatenate([x[:, 128 * ((k - h) % 4):128 * ((k - h) % 4) + 128] for k in range(4)], axis=1)
            e = jnp.exp2(dot(lhs, w, NT) * SCALE)
            total = e if total is None else total + e
    return total * jnp.exp2(dot(left, right, NT))


def lead_kernel(lead_ref, r4, lead_k):
    n = lead_ref.shape[0]

    def columns(c, _):
        o = pl.multiple_of(c * 256, 256)
        cols = pl.ds(o, 256)
        roll_into(lead_ref, o, r4)
        right = jnp.roll(lead_ref[cols, F:].astype(f32), 64, axis=1).astype(bf16)

        def above(m, _):
            rows = pl.ds(pl.multiple_of(m * 256, 256), 256)
            k = tile(lead_ref[rows, :], lambda r: r4[r, cols, :], right)
            i = m * 256 + lax.broadcasted_iota(jnp.int32, (256, 256), 0)
            j = o + lax.broadcasted_iota(jnp.int32, (256, 256), 1)
            k = k + jnp.where(i == j, RIDGE, 0.0)
            lead_k[rows, cols] = k
            lead_k[cols, rows] = k.T
            return 0

        lax.fori_loop(0, c + 1, above, 0)
        return 0

    lax.fori_loop(0, n // 256, columns, 0)


def lead_block(lead):
    n = lead.shape[0]
    return pl.pallas_call(
        lead_kernel,
        out_shape=(jax.ShapeDtypeStruct((4, n, F), bf16), jax.ShapeDtypeStruct((n, n), f32)),
        in_specs=[VMEM],
        out_specs=(VMEM, VMEM),
        compiler_params=pltpu.CompilerParams(vmem_limit_bytes=ROOM),
    )(lead)


def sub_row(y, k):
    return jnp.broadcast_to(y[k:k + 1, :], (8, 128))


def lane_col(y, k):
    return jnp.broadcast_to(y[:, k:k + 1], (8, 128))


def tree(terms):
    while len(terms) > 1:
        terms = [terms[i] + terms[i + 1] for i in range(0, len(terms), 2)]
    return terms[0]


def factor_steps(d, out):
    sub = lax.broadcasted_iota(jnp.int32, (8, 128), 0)
    lane = lax.broadcasted_iota(jnp.int32, (8, 128), 1)
    s = [d[8 * b:8 * b + 8] for b in range(16)]
    v = [jnp.where(lane == sub + 8 * b, 1.0, 0.0).astype(f32) for b in range(16)]
    for b in range(16):
        r, w = s[b], v[b]
        cols = [lane_col(r, 8 * b + k) for k in range(8)]
        x = jnp.zeros((8, 128), f32)
        for k in range(0, 8, 2):
            p11, p12, p22 = sub_row(cols[k], k), sub_row(cols[k + 1], k), sub_row(cols[k + 1], k + 1)
            det = p11 * p22 - p12 * p12
            rd = 1.0 / det
            m1 = jnp.where(sub == k, -1.0, jnp.where(sub == k + 1, 0.0, cols[k]))
            m2 = jnp.where(sub == k, 0.0, jnp.where(sub == k + 1, -1.0, cols[k + 1]))
            pair = (sub == k) | (sub == k + 1)

            def step(y):
                y1, y2 = sub_row(y, k), sub_row(y, k + 1)
                z1 = (p22 * y1 - p12 * y2) * rd
                z2 = (p11 * y2 - p12 * y1) * rd
                return (jnp.where(pair, 0.0, y) - m1 * z1) - m2 * z2, z2

            x = jnp.where(sub == k, w * lax.rsqrt(p11), x)
            r, _ = step(r)
            w, z = step(w)
            x = jnp.where(sub == k + 1, z * (det * lax.rsqrt(det * p11)), x)
            for j in range(k + 2, 8):
                cols[j], _ = step(cols[j])
            yield
        out.append(x)
        rk = [sub_row(r, k) for k in range(8)]
        wk = [sub_row(w, k) for k in range(8)]
        for i in range(b + 1, 16):
            c = [lane_col(s[i], 8 * b + k) for k in range(8)]
            s[i] = s[i] - tree([c[k] * rk[k] for k in range(8)])
            v[i] = v[i] - tree([c[k] * wk[k] for k in range(8)])


def main_kernel(rows_ref, cols_ref, lead_ref, r4, lead_k, out, c_ref, xh, xl, bh, bl, dref, r4c, aux, krh, krl, kch,
                kcl, ktr, acc, ph, plo, zh, zl):
    p = lax.axis_index("row")
    q = lax.axis_index("col")
    n = lead_ref.shape[0]
    for c in range(n // 256):
        aux[c * 256:c * 256 + 256, :] = jnp.roll(
            lead_ref[c * 256:c * 256 + 256, F:].astype(f32), 64, axis=1).astype(bf16)
    for c in range(cols_ref.shape[0] // 256):
        roll_into(cols_ref, c * 256, r4c)
        aux[n + c * 256:n + c * 256 + 256, :] = jnp.roll(
            cols_ref[c * 256:c * 256 + 256, F:].astype(f32), 64, axis=1).astype(bf16)
    c_ref[:256, :] = jnp.zeros((256, n), f32)
    c_ref[256:, :] = lead_k[...]
    bh[...] = jnp.zeros_like(bh)
    bl[...] = jnp.zeros_like(bl)
    dref[...] = lead_k[:256, :256]
    ri = lax.broadcasted_iota(jnp.int32, (256, 256), 0)
    ci = lax.broadcasted_iota(jnp.int32, (256, 256), 1)
    eye = jnp.where(ri == ci, 1.0, 0.0).astype(f32)

    def blk(k):
        return pl.ds(pl.multiple_of(k * 256, 256), 256)

    def cs(k):
        return pl.ds(k * 256, 256)

    def k_tile(t, left_ref, lo, rolled, ro, auxo, store):
        lhs = left_ref[lo, :F]
        for r in range(4):
            for h in range(4):
                x = rolled[r, ro, :]
                w = jnp.concatenate([x[:, 128 * ((k - h) % 4):128 * ((k - h) % 4) + 128] for k in range(4)], axis=1)
                e = jnp.exp2(dot(lhs, w, NT) * SCALE)
                if r + h == 0:
                    acc[t] = e
                else:
                    acc[t] = acc[t] + e
                yield
        lane = lax.broadcasted_iota(jnp.int32, (256, 128), 1)
        left = jnp.where(lane < 64, left_ref[lo, F:].astype(f32), 0.0).astype(bf16)
        store(acc[t] * jnp.exp2(dot(left, aux[auxo, :], NT)))
        yield

    def solve_row(g, prev):
        x = (bh[...], bl[...])
        for c in range(4):
            r = jnp.where(jnp.int32(c) == g - 1, eye, c_ref[blk(g), cs(c)])
            xh[blk(g), cs(c)], xl[blk(g), cs(c)] = split(dot3(x, split(r), NN))
            yield

    def update(g, prev):
        for r in range(3):
            i = lax.rem(g + r, 4)
            keep = jnp.where(r < 4 - g, 1.0, 0.0).astype(f32)
            f = split(dot3(split(c_ref[blk(i + 1), blk(prev)] * keep), (bh[...], bl[...]), NT))
            yield
            for c in range(4):
                old = jnp.where(jnp.int32(c) == g - 1, 0.0, c_ref[blk(i + 1), cs(c)])
                c_ref[blk(i + 1), cs(c)] = old - dot3(f, (xh[blk(g), cs(c)], xl[blk(g), cs(c)]), NN)
                yield

    def outer(g, _):
        prev = jnp.maximum(g - 1, 0)
        nxt = jnp.minimum(g + 1, 3)

        def work():
            yield from solve_row(g, prev)
            yield from update(g, prev)
            for m in range(4):
                def store(k, m=m):
                    k = k + jnp.where((ri + m * 256 < 128) & (ri + (m * 256 + p * 128) == ci + g * 256), RIDGE, 0.0)
                    krh[cs(m), blk(g)], krl[cs(m), blk(g)] = split(k)

                yield from k_tile(m % 2, rows_ref, cs(m), r4, blk(g), blk(g), store)
            for m in range(2):
                def store(k, m=m):
                    kch[cs(m), blk(g)], kcl[cs(m), blk(g)] = split(k)

                yield from k_tile(m % 2, cols_ref, cs(m), r4, blk(g), blk(g), store)
            for c in range(2):
                def store(k, c=c):
                    i, j = ri + g * 256, ci + c * 256
                    same = ((i >> 7) == (j >> 6)) & (p * 128 + (i & 127) == q * 64 + (j & 63))
                    k = k + jnp.where(same, RIDGE, 0.0)
                    ktr[blk(g), cs(c)] = jnp.where(j < 64, 0.0, k)

                yield from k_tile(c % 2, rows_ref, blk(g), r4c, cs(c), cs(4 + c), store)

        todo = work()
        credit = [0.0]

        def fill(amount):
            credit[0] += amount
            while credit[0] >= 1.0:
                credit[0] -= 1.0
                next(todo, None)

        per = 148.0 / 128.0
        d00 = dref[:128, :128]
        d10 = dref[128:, :128]
        d11 = dref[128:, 128:]
        out0, out1 = [], []
        for _s in factor_steps(d00, out0):
            fill(per)
        x0 = jnp.concatenate(out0, axis=0)
        x0s = split(x0)
        l10 = split(dot3(split(d10), x0s, NT))
        fill(2)
        d11 = d11 - dot3(l10, l10, NT)
        fill(2)
        g10 = split(dot3(l10, x0s, NN))
        for _s in factor_steps(d11, out1):
            fill(per)
        for _s in todo:
            pass
        x1 = jnp.concatenate(out1, axis=0)
        x10 = -dot3(split(x1), g10, NN)
        bh[:128, :128], bl[:128, :128] = x0s
        bh[128:, :128], bl[128:, :128] = split(x10)
        bh[128:, 128:], bl[128:, 128:] = split(x1)
        f = split(dot3(split(c_ref[blk(nxt + 1), blk(g)]), (bh[...], bl[...]), NT))
        dref[...] = c_ref[blk(nxt + 1), blk(nxt)] - dot3(f, f, NT)
        return 0

    lax.fori_loop(0, 4, outer, 0)
    for _s in solve_row(4, 3):
        pass

    def pcols(m, _):
        o = pl.ds(pl.multiple_of(m * 256, 256), 256)
        for j in range(0, n, 256):
            w = j + 256
            a = dot3((kch[o, :w], kcl[o, :w]), (xh[j + 256:w + 256, :w], xl[j + 256:w + 256, :w]), NT)
            ph[o, j:w], plo[o, j:w] = split(a)
        for j in range(0, n, 256):
            w = j + 256
            a = dot3((ph[o, j:], plo[o, j:]), (xh[j + 256:, j:w], xl[j + 256:, j:w]), NN)
            zh[o, j:w], zl[o, j:w] = split(a)
        return 0

    lax.fori_loop(0, cols_ref.shape[0] // 256, pcols, 0)
    first = pl.ds(pl.multiple_of(q * 64 + 256, 64), 64)
    keep = lax.broadcasted_iota(jnp.int32, (64, n), 1) <= q * 64 + lax.broadcasted_iota(jnp.int32, (64, n), 0)
    zh[:64, :] = jnp.where(keep, -xh[first, :].astype(f32), 0.0).astype(bf16)
    zl[:64, :] = jnp.where(keep, -xl[first, :].astype(f32), 0.0).astype(bf16)

    def last(m, _):
        o = pl.ds(pl.multiple_of(m * 256, 256), 256)
        out[o, :] = ktr[o, :] - dot3((krh[o, :], krl[o, :]), (zh[...], zl[...]), NT)
        return 0

    lax.fori_loop(0, rows_ref.shape[0] // 256, last, 0)


def main(rows, cols, lead, r4, lead_k):
    n, c, w = rows.shape[0], cols.shape[0], lead.shape[0]
    v = pltpu.VMEM
    return pl.pallas_call(
        main_kernel,
        out_shape=jax.ShapeDtypeStruct((n, c), f32),
        in_specs=[VMEM] * 5,
        out_specs=VMEM,
        scratch_shapes=[
            v((w + 256, w), f32), v((w + 256, w), bf16), v((w + 256, w), bf16), v((256, 256), bf16),
            v((256, 256), bf16), v((256, 256), f32), v((4, c, F), bf16), v((w + c, 128), bf16),
            v((n, w), bf16), v((n, w), bf16), v((c, w), bf16), v((c, w), bf16), v((n, c), f32), v((2, 256, 256), f32),
            v((c, w), bf16), v((c, w), bf16), v((c, w), bf16), v((c, w), bf16),
        ],
        compiler_params=pltpu.CompilerParams(vmem_limit_bytes=ROOM),
    )(rows, cols, lead, r4, lead_k)


def per_device(pool, ids, rot):
    ext = prep(pool, ids, rot)
    rows, cols, lead = exchange(ext)
    r4, lead_k = lead_block(lead)
    return main(rows, cols, lead, r4, lead_k)


def solution(mesh):
    return jax.shard_map(
        per_device,
        mesh=mesh,
        in_specs=(P("row", None), P("row", None), P("row")),
        out_specs=P("row", "col"),
        check_vma=False,
    )
```

```python
import functools
import math

import jax
import jax.numpy as jnp
import numpy as np
from jax import lax
from jax.experimental import pallas as pl
from jax.experimental.pallas import tpu as pltpu
from jax.sharding import PartitionSpec as P

MESH = pl.DeviceIdType.MESH
f32 = jnp.float32
bf16 = jnp.bfloat16

ROTS = 16
SHARPNESS = 2.0
RIDGE = 0.1
F = 512
E = 640
G = 8
Q = 16
LOG2E = math.log2(math.e)
SCALE = 2.0 * LOG2E / F
VMEM = pl.BlockSpec(memory_space=pltpu.VMEM)
ROOM = 56 * 2**20


def split3(x):
    a = x.astype(bf16)
    x = x - a.astype(f32)
    b = x.astype(bf16)
    return a, b, (x - b.astype(f32)).astype(bf16)


def split(x):
    hi = x.astype(bf16)
    return hi, (x - hi.astype(f32)).astype(bf16)


def dot(a, b, dims):
    return lax.dot_general(a, b, (dims, ((), ())), preferred_element_type=f32)


def dot3(a, b, dims):
    ah, al = a
    bh, bl = b
    return dot(ah, bh, dims) + (dot(ah, bl, dims) + dot(al, bh, dims))


NT = ((1,), (1,))
NN = ((1,), (0,))
TN = ((0,), (0,))


def bin_table():
    angle = 2.0 * np.pi * np.arange(ROTS) / ROTS
    table = np.zeros((128, 128), np.float64)
    root = math.sqrt(SHARPNESS * LOG2E)
    for first, values in ((6, root * np.cos(angle)), (12, root * np.sin(angle))):
        parts, rest = [], values
        for _ in range(3):
            part = rest.astype(np.float32).astype(jnp.bfloat16).astype(np.float64)
            parts.append(part)
            rest = rest - part
        for lane, (left, right) in enumerate(((0, 0), (0, 1), (1, 0), (0, 2), (1, 1), (2, 0))):
            table[:ROTS, first + lane] = parts[left]
            table[:ROTS, 64 + first + lane] = parts[right]
    table[:ROTS, 3:6] = 1.0
    table[:ROTS, 64:67] = 1.0
    return table.astype(np.float32).astype(jnp.bfloat16)


def roll_into(src, o, r4):
    feats = src[pl.ds(o, 256), :F].astype(f32)
    for r in range(4):
        r4[r, pl.ds(o, 256), :] = (jnp.roll(feats, 32 * r, axis=1) if r else feats).astype(bf16)


def right_lanes(src, o):
    return jnp.roll(src[pl.ds(o, 256), F:].astype(f32), 64, axis=1).astype(bf16)


def tile(rows, rolled, right):
    lane = lax.broadcasted_iota(jnp.int32, (rows.shape[0], 128), 1)
    left = jnp.where(lane < 64, rows[:, F:].astype(f32), 0.0).astype(bf16)
    lhs = rows[:, :F]
    total = None
    for r in range(4):
        x = rolled(r)
        for h in range(4):
            w = jnp.concatenate([x[:, 128 * ((k - h) % 4):128 * ((k - h) % 4) + 128] for k in range(4)], axis=1)
            e = jnp.exp2(dot(lhs, w, NT) * SCALE)
            total = e if total is None else total + e
    return total * jnp.exp2(dot(left, right, NT))


def exchange_kernel(pool_ref, ids_ref, rot_ref, table_ref, rows_ref, cols_ref, r4, aux, lead_k, ext_ref, lead_ref,
                    local, s_col, r_first, r_col, s_lead, r_lead, s_leadf, r_leadf, s_row, r_row, s_rowf, r_rowf,
                    s_tile, r_tile):
    p = lax.axis_index("row")
    q = lax.axis_index("col")
    core = lax.rem(q, 2)
    sibling = (p, q + 1 - 2 * core)
    n = pool_ref.shape[0]
    barrier = pltpu.get_barrier_semaphore()
    rows_to = [(lax.rem(p + d, G), q) for d in range(1, G)]
    cols_to = [(p, lax.rem(q + 2 * d, Q)) for d in range(1, Q // 2)]
    for device in rows_to + cols_to + [sibling]:
        pl.semaphore_signal(barrier, inc=1, device_id=device, device_id_type=MESH)

    def features(k):
        o = pl.ds(pl.multiple_of(k * 128, 128), 128)
        lane = lax.broadcasted_iota(jnp.int32, (128, 128), 1)
        down = jnp.broadcast_to(ids_ref[pl.ds(k, 1), :].astype(f32), (128, 128)).T.astype(jnp.int32)
        bins = jnp.broadcast_to(rot_ref[pl.ds(k, 1), :].astype(f32), (128, 128)).T.astype(jnp.int32)
        pick = jnp.concatenate(
            [jnp.where(down == lane + c * 128, 1.0, 0.0).astype(bf16) for c in range(n // 128)], axis=1)
        feats = dot(pick, pool_ref[...], NN)
        norm = jnp.sum(feats * feats, axis=1, keepdims=True)
        a = jnp.broadcast_to(norm * (-LOG2E / F) - (SHARPNESS * LOG2E / 2.0 + 2.0), (128, 128))
        extra = dot(jnp.where(bins == lane, 1.0, 0.0).astype(bf16), table_ref[...], NN)
        for i, part in enumerate(split3(a)):
            extra = jnp.where((lane == i) | (lane == 64 + 3 + i), part.astype(f32), extra)
        ext_ref[o, :F] = feats.astype(bf16)
        ext_ref[o, F:] = extra.astype(bf16)

    def piece(k):
        return pl.ds(pl.multiple_of(k * 64, 64), 64)

    def copy(src, dst, send, recv, device):
        return pltpu.make_async_remote_copy(
            src_ref=src, dst_ref=dst, send_sem=send, recv_sem=recv, device_id=device, device_id_type=MESH)

    def arrived(ref, sem):
        copy(ref, ref, s_col.at[0], sem, sibling).wait_recv()

    first = lax.div(q, 2)
    features(first)
    pl.semaphore_wait(barrier, G - 1 + Q // 2)
    own = piece(q)
    starts = [copy(ext_ref.at[own, :], lead_ref.at[own, :], s_col.at[d - 1], r_first.at[0], rows_to[d - 1])
              for d in range(1, G)]

    @pl.when(p == 0)
    def _():
        for c in starts:
            c.start()

    def others(i, _):
        features(lax.rem(first + i, n // 128))
        return 0

    lax.fori_loop(1, n // 128, others, 0)

    @pl.when(p == 0)
    def _():
        c = pltpu.make_async_copy(ext_ref.at[own, :], lead_ref.at[own, :], local.at[0])
        c.start()
        c.wait()

    @pl.when(p != 0)
    def _():
        arrived(lead_ref.at[own, :], r_first.at[0])

    leads = [copy(lead_ref.at[own, :], lead_ref.at[own, :], s_lead.at[d], r_leadf.at[d] if d == 0 else r_lead.at[d - 1],
                  sibling if d == 0 else cols_to[d - 1]) for d in range(Q // 2)]
    for c in leads[1:] + leads[:1]:
        c.start()
    half = [copy(ext_ref.at[piece(2 * to[0] + core), :], rows_ref.at[piece(2 * p + core), :], s_row.at[d], r_row.at[d],
                 to) for d, to in enumerate(rows_to)]
    cols = [copy(ext_ref.at[own, :], cols_ref.at[piece(p), :], s_col.at[d], r_col.at[d], to)
            for d, to in enumerate(rows_to)]
    own_rows = pltpu.make_async_copy(
        ext_ref.at[pl.ds(pl.multiple_of(p * 128, 128), 128), :], rows_ref.at[pl.ds(pl.multiple_of(p * 128, 128), 128), :],
        local.at[1])
    own_rows.start()
    own_cols = pltpu.make_async_copy(lead_ref.at[own, :], cols_ref.at[piece(0), :], local.at[2])
    own_cols.start()
    own_piece = pltpu.make_async_copy(ext_ref.at[own, :], cols_ref.at[piece(p), :], local.at[0])

    @pl.when(p != 0)
    def _():
        own_piece.start()

    passed = []
    for d in range(1, Q // 2):
        at = lead_ref.at[piece(lax.rem(q - 2 * d + Q, Q)), :]
        arrived(at, r_lead.at[d - 1])
        c = copy(at, at, s_leadf.at[d - 1], r_leadf.at[d], sibling)
        c.start()
        passed.append(c)
    for c in half:
        c.start()

    @pl.when(p != 0)
    def _():
        for c in cols:
            c.start()

    for d in range(Q // 2):
        at = lead_ref.at[piece(lax.rem(sibling[1] - 2 * d + Q, Q)), :]
        arrived(at, r_leadf.at[d])

    def turn(c, _):
        o = pl.multiple_of(c * 256, 256)
        roll_into(lead_ref, o, r4)
        aux[pl.ds(o, 256), :] = right_lanes(lead_ref, o)
        return 0

    lax.fori_loop(0, n // 256, turn, 0)

    def blk(k):
        return pl.ds(pl.multiple_of(k * 256, 256), 256)

    def lead_tile(m, c):
        k = tile(lead_ref[blk(m), :], lambda r: r4[r, blk(c), :], aux[blk(c), :])
        i = m * 256 + lax.broadcasted_iota(jnp.int32, (256, 256), 0)
        j = c * 256 + lax.broadcasted_iota(jnp.int32, (256, 256), 1)
        return k + jnp.where(i == j, RIDGE, 0.0)

    def swap(k, m, c):
        at = lead_k.at[blk(m), blk(c)]
        return copy(at, at, s_tile.at[k], r_tile.at[k], sibling)

    def place(t, side):
        above = (0, 0, 1)[t] + side * ((0, 1, 2)[t] - (0, 0, 1)[t])
        right = (1, 2, 2)[t] + side * (3 - (1, 2, 2)[t])
        return above, right

    swaps, theirs = [], []
    for t in range(2):
        m = t + 2 * core
        lead_k[blk(m), blk(m)] = lead_tile(m, m)
        c = swap(t, m, m)
        c.start()
        swaps.append(c)
        theirs.append((t, t + 2 * (1 - core), t + 2 * (1 - core)))
    rowsf = []
    for t in range(3):
        m, c = place(t, core)
        k = lead_tile(m, c)
        lead_k[blk(m), blk(c)] = k
        lead_k[blk(c), blk(m)] = k.T
        for s, (a, b) in enumerate(((m, c), (c, m))):
            w = swap(2 + 2 * t + s, a, b)
            w.start()
            swaps.append(w)
        a, b = place(t, 1 - core)
        theirs += [(2 + 2 * t, a, b), (3 + 2 * t, b, a)]
        if t == 1:
            for d in range(G - 1):
                at = rows_ref.at[piece(2 * lax.rem(p - d - 1 + G, G) + core), :]
                arrived(at, r_row.at[d])
                w = copy(at, at, s_rowf.at[d], r_rowf.at[d], sibling)
                w.start()
                rowsf.append(w)
    own_rows.wait()
    own_cols.wait()

    @pl.when(p != 0)
    def _():
        own_piece.wait()
    for c in leads + passed + half + rowsf + swaps + cols:
        c.wait_send()
    for d in range(G - 1):
        arrived(rows_ref.at[piece(2 * lax.rem(p - d - 1 + G, G) + 1 - core), :], r_rowf.at[d])
        sender = lax.rem(p - d - 1 + G, G)

        @pl.when(sender != 0)
        def _():
            arrived(cols_ref.at[piece(sender), :], r_col.at[d])
    for k, m, c in theirs:
        arrived(lead_k.at[blk(m), blk(c)], r_tile.at[k])


def exchange(pool, ids, rot):
    n = pool.shape[0]
    dma = pltpu.SemaphoreType.DMA
    s = jax.ShapeDtypeStruct
    return pl.pallas_call(
        exchange_kernel,
        out_shape=(s((n, E), bf16), s((n // 2, E), bf16), s((4, n, F), bf16), s((n, 128), bf16), s((n, n), f32)),
        in_specs=[VMEM] * 4,
        out_specs=(VMEM,) * 5,
        scratch_shapes=[
            pltpu.VMEM((n, E), bf16), pltpu.VMEM((n, E), bf16), dma((3,)), dma((G - 1,)), dma((1,)), dma((G - 1,)),
            dma((8,)), dma((7,)), dma((7,)), dma((8,)), dma((G - 1,)), dma((G - 1,)), dma((G - 1,)), dma((G - 1,)),
            dma((8,)), dma((8,)),
        ],
        compiler_params=pltpu.CompilerParams(collective_id=0, has_side_effects=True, vmem_limit_bytes=ROOM),
    )(pool, ids.reshape(n // 128, 128), rot.reshape(n // 128, 128), jnp.asarray(bin_table()))


def sub_row(y, k):
    return jnp.broadcast_to(y[k:k + 1, :], (8, 128))


def lane_col(y, k):
    return jnp.broadcast_to(y[:, k:k + 1], (8, 128))


def tree(terms):
    while len(terms) > 1:
        terms = [terms[i] + terms[i + 1] for i in range(0, len(terms), 2)]
    return terms[0]


def factor_steps(d, out):
    sub = lax.broadcasted_iota(jnp.int32, (8, 128), 0)
    lane = lax.broadcasted_iota(jnp.int32, (8, 128), 1)
    s = [d[8 * b:8 * b + 8] for b in range(16)]
    v = [jnp.where(lane == sub + 8 * b, 1.0, 0.0).astype(f32) for b in range(16)]
    for b in range(16):
        r, w = s[b], v[b]
        cols = [lane_col(r, 8 * b + k) for k in range(8)]
        x = jnp.zeros((8, 128), f32)
        for k in range(0, 8, 2):
            p11, p12, p22 = sub_row(cols[k], k), sub_row(cols[k + 1], k), sub_row(cols[k + 1], k + 1)
            det = p11 * p22 - p12 * p12
            rd = 1.0 / det
            m1 = jnp.where(sub == k, -1.0, jnp.where(sub == k + 1, 0.0, cols[k]))
            m2 = jnp.where(sub == k, 0.0, jnp.where(sub == k + 1, -1.0, cols[k + 1]))
            pair = (sub == k) | (sub == k + 1)

            def step(y):
                y1, y2 = sub_row(y, k), sub_row(y, k + 1)
                z1 = (p22 * y1 - p12 * y2) * rd
                z2 = (p11 * y2 - p12 * y1) * rd
                return (jnp.where(pair, 0.0, y) - m1 * z1) - m2 * z2, z2

            x = jnp.where(sub == k, w * lax.rsqrt(p11), x)
            r, _ = step(r)
            w, z = step(w)
            x = jnp.where(sub == k + 1, z * (det * lax.rsqrt(det * p11)), x)
            for j in range(k + 2, 8):
                cols[j], _ = step(cols[j])
            yield
        out.append(x)
        rk = [sub_row(r, k) for k in range(8)]
        wk = [sub_row(w, k) for k in range(8)]
        for i in range(b + 1, 16):
            c = [lane_col(s[i], 8 * b + k) for k in range(8)]
            s[i] = s[i] - tree([c[k] * rk[k] for k in range(8)])
            v[i] = v[i] - tree([c[k] * wk[k] for k in range(8)])


def main_kernel(rows_ref, cols_ref, r4, lead_aux, lead_k, out, c_ref, xh, xl, bh, bl, dref, r4c, aux, krh, krl, kch,
                kcl, ktr, acc, ph, plo, zh, zl):
    p = lax.axis_index("row")
    q = lax.axis_index("col")
    n = lead_k.shape[0]
    aux[:n, :] = lead_aux[...]
    for c in range(cols_ref.shape[0] // 256):
        roll_into(cols_ref, c * 256, r4c)
        aux[n + c * 256:n + c * 256 + 256, :] = right_lanes(cols_ref, c * 256)
    c_ref[:256, :] = jnp.zeros((256, n), f32)
    c_ref[256:, :] = lead_k[...]
    bh[...] = jnp.zeros_like(bh)
    bl[...] = jnp.zeros_like(bl)
    dref[...] = lead_k[:256, :256]
    ri = lax.broadcasted_iota(jnp.int32, (256, 256), 0)
    ci = lax.broadcasted_iota(jnp.int32, (256, 256), 1)
    eye = jnp.where(ri == ci, 1.0, 0.0).astype(f32)

    def blk(k):
        return pl.ds(pl.multiple_of(k * 256, 256), 256)

    def cs(k):
        return pl.ds(k * 256, 256)

    def k_tile(t, left_ref, lo, rolled, ro, auxo, store):
        lhs = left_ref[lo, :F]
        for r in range(4):
            for h in range(4):
                x = rolled[r, ro, :]
                w = jnp.concatenate([x[:, 128 * ((k - h) % 4):128 * ((k - h) % 4) + 128] for k in range(4)], axis=1)
                e = jnp.exp2(dot(lhs, w, NT) * SCALE)
                if r + h == 0:
                    acc[t] = e
                else:
                    acc[t] = acc[t] + e
                yield
        lane = lax.broadcasted_iota(jnp.int32, (256, 128), 1)
        left = jnp.where(lane < 64, left_ref[lo, F:].astype(f32), 0.0).astype(bf16)
        store(acc[t] * jnp.exp2(dot(left, aux[auxo, :], NT)))
        yield

    def solve_row(g, prev):
        x = (bh[...], bl[...])
        for c in range(4):
            r = jnp.where(jnp.int32(c) == g - 1, eye, c_ref[blk(g), cs(c)])
            xh[blk(g), cs(c)], xl[blk(g), cs(c)] = split(dot3(x, split(r), NN))
            yield

    def update(g, prev):
        for r in range(3):
            i = lax.rem(g + r, 4)
            keep = jnp.where(r < 4 - g, 1.0, 0.0).astype(f32)
            f = split(dot3(split(c_ref[blk(i + 1), blk(prev)] * keep), (bh[...], bl[...]), NT))
            yield
            for c in range(4):
                old = jnp.where(jnp.int32(c) == g - 1, 0.0, c_ref[blk(i + 1), cs(c)])
                c_ref[blk(i + 1), cs(c)] = old - dot3(f, (xh[blk(g), cs(c)], xl[blk(g), cs(c)]), NN)
                yield

    def outer(g, _):
        prev = jnp.maximum(g - 1, 0)
        nxt = jnp.minimum(g + 1, 3)

        def work():
            yield from solve_row(g, prev)
            yield from update(g, prev)
            for m in range(4):
                def store(k, m=m):
                    k = k + jnp.where((ri + m * 256 < 128) & (ri + (m * 256 + p * 128) == ci + g * 256), RIDGE, 0.0)
                    krh[cs(m), blk(g)], krl[cs(m), blk(g)] = split(k)

                yield from k_tile(m % 2, rows_ref, cs(m), r4, blk(g), blk(g), store)
            for m in range(2):
                def store(k, m=m):
                    kch[cs(m), blk(g)], kcl[cs(m), blk(g)] = split(k)

                yield from k_tile(m % 2, cols_ref, cs(m), r4, blk(g), blk(g), store)
            for c in range(2):
                def store(k, c=c):
                    i, j = ri + g * 256, ci + c * 256
                    same = ((i >> 7) == (j >> 6)) & (p * 128 + (i & 127) == q * 64 + (j & 63))
                    k = k + jnp.where(same, RIDGE, 0.0)
                    ktr[blk(g), cs(c)] = jnp.where(j < 64, 0.0, k)

                yield from k_tile(c % 2, rows_ref, blk(g), r4c, cs(c), cs(4 + c), store)

        todo = work()
        credit = [0.0]

        def fill(amount):
            credit[0] += amount
            while credit[0] >= 1.0:
                credit[0] -= 1.0
                next(todo, None)

        per = 148.0 / 128.0
        d00 = dref[:128, :128]
        d10 = dref[128:, :128]
        d11 = dref[128:, 128:]
        out0, out1 = [], []
        for _s in factor_steps(d00, out0):
            fill(per)
        x0 = jnp.concatenate(out0, axis=0)
        x0s = split(x0)
        l10 = split(dot3(split(d10), x0s, NT))
        fill(2)
        d11 = d11 - dot3(l10, l10, NT)
        fill(2)
        g10 = split(dot3(l10, x0s, NN))
        for _s in factor_steps(d11, out1):
            fill(per)
        for _s in todo:
            pass
        x1 = jnp.concatenate(out1, axis=0)
        x10 = -dot3(split(x1), g10, NN)
        bh[:128, :128], bl[:128, :128] = x0s
        bh[128:, :128], bl[128:, :128] = split(x10)
        bh[128:, 128:], bl[128:, 128:] = split(x1)
        f = split(dot3(split(c_ref[blk(nxt + 1), blk(g)]), (bh[...], bl[...]), NT))
        dref[...] = c_ref[blk(nxt + 1), blk(nxt)] - dot3(f, f, NT)
        return 0

    lax.fori_loop(0, 4, outer, 0)
    for _s in solve_row(4, 3):
        pass

    def pcols(m, _):
        o = pl.ds(pl.multiple_of(m * 256, 256), 256)
        for j in range(0, n, 256):
            w = j + 256
            a = dot3((kch[o, :w], kcl[o, :w]), (xh[j + 256:w + 256, :w], xl[j + 256:w + 256, :w]), NT)
            ph[o, j:w], plo[o, j:w] = split(a)
        for j in range(0, n, 256):
            w = j + 256
            a = dot3((ph[o, j:], plo[o, j:]), (xh[j + 256:, j:w], xl[j + 256:, j:w]), NN)
            zh[o, j:w], zl[o, j:w] = split(a)
        return 0

    lax.fori_loop(0, cols_ref.shape[0] // 256, pcols, 0)
    first = pl.ds(pl.multiple_of(q * 64 + 256, 64), 64)
    keep = lax.broadcasted_iota(jnp.int32, (64, n), 1) <= q * 64 + lax.broadcasted_iota(jnp.int32, (64, n), 0)
    zh[:64, :] = jnp.where(keep, -xh[first, :].astype(f32), 0.0).astype(bf16)
    zl[:64, :] = jnp.where(keep, -xl[first, :].astype(f32), 0.0).astype(bf16)

    def last(m, _):
        o = pl.ds(pl.multiple_of(m * 256, 256), 256)
        out[o, :] = ktr[o, :] - dot3((krh[o, :], krl[o, :]), (zh[...], zl[...]), NT)
        return 0

    lax.fori_loop(0, rows_ref.shape[0] // 256, last, 0)


def main(rows, cols, r4, aux, lead_k):
    n, c, w = rows.shape[0], cols.shape[0], lead_k.shape[0]
    v = pltpu.VMEM
    return pl.pallas_call(
        main_kernel,
        out_shape=jax.ShapeDtypeStruct((n, c), f32),
        in_specs=[VMEM] * 5,
        out_specs=VMEM,
        scratch_shapes=[
            v((w + 256, w), f32), v((w + 256, w), bf16), v((w + 256, w), bf16), v((256, 256), bf16),
            v((256, 256), bf16), v((256, 256), f32), v((4, c, F), bf16), v((w + c, 128), bf16),
            v((n, w), bf16), v((n, w), bf16), v((c, w), bf16), v((c, w), bf16), v((n, c), f32), v((2, 256, 256), f32),
            v((c, w), bf16), v((c, w), bf16), v((c, w), bf16), v((c, w), bf16),
        ],
        compiler_params=pltpu.CompilerParams(vmem_limit_bytes=ROOM),
    )(rows, cols, r4, aux, lead_k)


def per_device(pool, ids, rot):
    return main(*exchange(pool, ids, rot))


def solution(mesh):
    return jax.shard_map(
        per_device,
        mesh=mesh,
        in_specs=(P("row", None), P("row", None), P("row")),
        out_specs=P("row", "col"),
        check_vma=False,
    )
```

```python
import functools
import math

import jax
import jax.numpy as jnp
import numpy as np
from jax import lax
from jax.experimental import pallas as pl
from jax.experimental.pallas import tpu as pltpu
from jax.sharding import PartitionSpec as P

MESH = pl.DeviceIdType.MESH
f32 = jnp.float32
bf16 = jnp.bfloat16

ROTS = 16
SHARPNESS = 2.0
RIDGE = 0.1
F = 512
E = 640
G = 8
Q = 16
LOG2E = math.log2(math.e)
SCALE = 2.0 * LOG2E / F
VMEM = pl.BlockSpec(memory_space=pltpu.VMEM)
ROOM = 56 * 2**20


def split3(x):
    a = x.astype(bf16)
    x = x - a.astype(f32)
    b = x.astype(bf16)
    return a, b, (x - b.astype(f32)).astype(bf16)


def split(x):
    hi = x.astype(bf16)
    return hi, (x - hi.astype(f32)).astype(bf16)


def dot(a, b, dims):
    return lax.dot_general(a, b, (dims, ((), ())), preferred_element_type=f32)


def dot3(a, b, dims):
    ah, al = a
    bh, bl = b
    return dot(ah, bh, dims) + (dot(ah, bl, dims) + dot(al, bh, dims))


NT = ((1,), (1,))
NN = ((1,), (0,))
TN = ((0,), (0,))


def bin_table():
    angle = 2.0 * np.pi * np.arange(ROTS) / ROTS
    table = np.zeros((128, 128), np.float64)
    root = math.sqrt(SHARPNESS * LOG2E)
    for first, values in ((6, root * np.cos(angle)), (12, root * np.sin(angle))):
        parts, rest = [], values
        for _ in range(3):
            part = rest.astype(np.float32).astype(jnp.bfloat16).astype(np.float64)
            parts.append(part)
            rest = rest - part
        for lane, (left, right) in enumerate(((0, 0), (0, 1), (1, 0), (0, 2), (1, 1), (2, 0))):
            table[:ROTS, first + lane] = parts[left]
            table[:ROTS, 64 + first + lane] = parts[right]
    table[:ROTS, 3:6] = 1.0
    table[:ROTS, 64:67] = 1.0
    return table.astype(np.float32).astype(jnp.bfloat16)


def roll_into(src, o, r4):
    feats = src[pl.ds(o, 256), :F].astype(f32)
    for r in range(4):
        r4[r, pl.ds(o, 256), :] = (jnp.roll(feats, 32 * r, axis=1) if r else feats).astype(bf16)


def right_lanes(src, o):
    return jnp.roll(src[pl.ds(o, 256), F:].astype(f32), 64, axis=1).astype(bf16)


def tile(rows, rolled, right):
    lane = lax.broadcasted_iota(jnp.int32, (rows.shape[0], 128), 1)
    left = jnp.where(lane < 64, rows[:, F:].astype(f32), 0.0).astype(bf16)
    lhs = rows[:, :F]
    total = None
    for r in range(4):
        x = rolled(r)
        for h in range(4):
            w = jnp.concatenate([x[:, 128 * ((k - h) % 4):128 * ((k - h) % 4) + 128] for k in range(4)], axis=1)
            e = jnp.exp2(dot(lhs, w, NT) * SCALE)
            total = e if total is None else total + e
    return total * jnp.exp2(dot(left, right, NT))


def sub_row(y, k):
    return jnp.broadcast_to(y[k:k + 1, :], (8, 128))


def lane_col(y, k):
    return jnp.broadcast_to(y[:, k:k + 1], (8, 128))


def tree(terms):
    while len(terms) > 1:
        terms = [terms[i] + terms[i + 1] for i in range(0, len(terms), 2)]
    return terms[0]


def factor_steps(d, out):
    sub = lax.broadcasted_iota(jnp.int32, (8, 128), 0)
    lane = lax.broadcasted_iota(jnp.int32, (8, 128), 1)
    s = [d[8 * b:8 * b + 8] for b in range(16)]
    v = [jnp.where(lane == sub + 8 * b, 1.0, 0.0).astype(f32) for b in range(16)]
    for b in range(16):
        r, w = s[b], v[b]
        cols = [lane_col(r, 8 * b + k) for k in range(8)]
        x = jnp.zeros((8, 128), f32)
        for k in range(0, 8, 2):
            p11, p12, p22 = sub_row(cols[k], k), sub_row(cols[k + 1], k), sub_row(cols[k + 1], k + 1)
            det = p11 * p22 - p12 * p12
            rd = 1.0 / det
            m1 = jnp.where(sub == k, -1.0, jnp.where(sub == k + 1, 0.0, cols[k]))
            m2 = jnp.where(sub == k, 0.0, jnp.where(sub == k + 1, -1.0, cols[k + 1]))
            pair = (sub == k) | (sub == k + 1)

            def step(y):
                y1, y2 = sub_row(y, k), sub_row(y, k + 1)
                z1 = (p22 * y1 - p12 * y2) * rd
                z2 = (p11 * y2 - p12 * y1) * rd
                return (jnp.where(pair, 0.0, y) - m1 * z1) - m2 * z2, z2

            x = jnp.where(sub == k, w * lax.rsqrt(p11), x)
            r, _ = step(r)
            w, z = step(w)
            x = jnp.where(sub == k + 1, z * (det * lax.rsqrt(det * p11)), x)
            for j in range(k + 2, 8):
                cols[j], _ = step(cols[j])
            yield
        out.append(x)
        rk = [sub_row(r, k) for k in range(8)]
        wk = [sub_row(w, k) for k in range(8)]
        for i in range(b + 1, 16):
            c = [lane_col(s[i], 8 * b + k) for k in range(8)]
            s[i] = s[i] - tree([c[k] * rk[k] for k in range(8)])
            v[i] = v[i] - tree([c[k] * wk[k] for k in range(8)])


def fused_kernel(pool_ref, ids_ref, rot_ref, table_ref, out, rows_ref, cols_ref, r4, aux, ext_ref, lead_ref, c_ref, xh,
                 xl, bh, bl, dref, r4c, krh, krl, kch, kcl, ktr, acc, ph, plo, zh, zl, local, s_col, r_first, r_col,
                 s_lead, r_lead, s_leadf, r_leadf, s_row, r_row, s_rowf, r_rowf, s_tile, r_tile, s_half, r_half):
    p = lax.axis_index("row")
    q = lax.axis_index("col")
    core = lax.rem(q, 2)
    sibling = (p, q + 1 - 2 * core)
    n = pool_ref.shape[0]
    barrier = pltpu.get_barrier_semaphore()
    rows_to = [(lax.rem(p + d, G), q) for d in range(1, G)]
    cols_to = [(p, lax.rem(q + 2 * d, Q)) for d in range(1, Q // 2)]
    for device in rows_to + cols_to + [sibling]:
        pl.semaphore_signal(barrier, inc=1, device_id=device, device_id_type=MESH)

    def features(k):
        o = pl.ds(pl.multiple_of(k * 128, 128), 128)
        lane = lax.broadcasted_iota(jnp.int32, (128, 128), 1)
        down = jnp.broadcast_to(ids_ref[pl.ds(k, 1), :].astype(f32), (128, 128)).T.astype(jnp.int32)
        bins = jnp.broadcast_to(rot_ref[pl.ds(k, 1), :].astype(f32), (128, 128)).T.astype(jnp.int32)
        pick = jnp.concatenate(
            [jnp.where(down == lane + c * 128, 1.0, 0.0).astype(bf16) for c in range(n // 128)], axis=1)
        feats = dot(pick, pool_ref[...], NN)
        norm = jnp.sum(feats * feats, axis=1, keepdims=True)
        a = jnp.broadcast_to(norm * (-LOG2E / F) - (SHARPNESS * LOG2E / 2.0 + 2.0), (128, 128))
        extra = dot(jnp.where(bins == lane, 1.0, 0.0).astype(bf16), table_ref[...], NN)
        for i, part in enumerate(split3(a)):
            extra = jnp.where((lane == i) | (lane == 64 + 3 + i), part.astype(f32), extra)
        ext_ref[o, :F] = feats.astype(bf16)
        ext_ref[o, F:] = extra.astype(bf16)

    def piece(k):
        return pl.ds(pl.multiple_of(k * 64, 64), 64)

    def copy(src, dst, send, recv, device):
        return pltpu.make_async_remote_copy(
            src_ref=src, dst_ref=dst, send_sem=send, recv_sem=recv, device_id=device, device_id_type=MESH)

    def arrived(ref, sem):
        copy(ref, ref, s_col.at[0], sem, sibling).wait_recv()

    first = lax.div(q, 2)
    features(first)
    pl.semaphore_wait(barrier, G - 1 + Q // 2)
    own = piece(q)
    starts = [copy(ext_ref.at[own, :], lead_ref.at[own, :], s_col.at[d - 1], r_first.at[0], rows_to[d - 1])
              for d in range(1, G)]

    @pl.when(p == 0)
    def _():
        for c in starts:
            c.start()

    def others(i, _):
        features(lax.rem(first + i, n // 128))
        return 0

    lax.fori_loop(1, n // 128, others, 0)

    half = [copy(ext_ref.at[piece(2 * to[0] + core), :], rows_ref.at[piece(2 * p + core), :], s_row.at[d], r_row.at[d],
                 to) for d, to in enumerate(rows_to)]
    cols = [copy(ext_ref.at[own, :], cols_ref.at[piece(p), :], s_col.at[d], r_col.at[d], to)
            for d, to in enumerate(rows_to)]
    for c in half:
        c.start()

    @pl.when(p != 0)
    def _():
        for c in cols:
            c.start()

    @pl.when(p == 0)
    def _():
        c = pltpu.make_async_copy(ext_ref.at[own, :], lead_ref.at[own, :], local.at[0])
        c.start()
        c.wait()

    @pl.when(p != 0)
    def _():
        arrived(lead_ref.at[own, :], r_first.at[0])

    leads = [copy(lead_ref.at[own, :], lead_ref.at[own, :], s_lead.at[d], r_leadf.at[d] if d == 0 else r_lead.at[d - 1],
                  sibling if d == 0 else cols_to[d - 1]) for d in range(Q // 2)]
    for c in leads[1:] + leads[:1]:
        c.start()
    own_rows = pltpu.make_async_copy(
        ext_ref.at[pl.ds(pl.multiple_of(p * 128, 128), 128), :], rows_ref.at[pl.ds(pl.multiple_of(p * 128, 128), 128), :],
        local.at[1])
    own_rows.start()
    own_cols = pltpu.make_async_copy(lead_ref.at[own, :], cols_ref.at[piece(0), :], local.at[2])
    own_cols.start()
    own_piece = pltpu.make_async_copy(ext_ref.at[own, :], cols_ref.at[piece(p), :], local.at[0])

    @pl.when(p != 0)
    def _():
        own_piece.start()

    passed = []
    for d in range(1, Q // 2):
        at = lead_ref.at[piece(lax.rem(q - 2 * d + Q, Q)), :]
        arrived(at, r_lead.at[d - 1])
        c = copy(at, at, s_leadf.at[d - 1], r_leadf.at[d], sibling)
        c.start()
        passed.append(c)
    for d in range(Q // 2):
        at = lead_ref.at[piece(lax.rem(sibling[1] - 2 * d + Q, Q)), :]
        arrived(at, r_leadf.at[d])

    def turn(c, _):
        o = pl.multiple_of(c * 256, 256)
        roll_into(lead_ref, o, r4)
        aux[pl.ds(o, 256), :] = right_lanes(lead_ref, o)
        return 0

    lax.fori_loop(0, n // 256, turn, 0)

    def blk(k):
        return pl.ds(pl.multiple_of(k * 256, 256), 256)

    def lead_tile(m, c):
        k = tile(lead_ref[blk(m), :], lambda r: r4[r, blk(c), :], aux[blk(c), :])
        i = m * 256 + lax.broadcasted_iota(jnp.int32, (256, 256), 0)
        j = c * 256 + lax.broadcasted_iota(jnp.int32, (256, 256), 1)
        return k + jnp.where(i == j, RIDGE, 0.0)

    def swap(k, m, c):
        at = c_ref.at[blk(m + 1), blk(c)]
        return copy(at, at, s_tile.at[k], r_tile.at[k], sibling)

    def place(t, side):
        above = (0, 0, 1)[t] + side * ((0, 1, 2)[t] - (0, 0, 1)[t])
        right = (1, 2, 2)[t] + side * (3 - (1, 2, 2)[t])
        return above, right

    swaps, theirs = [], []
    for t in range(2):
        m = t + 2 * core
        c_ref[blk(m + 1), blk(m)] = lead_tile(m, m)
        c = swap(t, m, m)
        c.start()
        swaps.append(c)
        theirs.append((t, t + 2 * (1 - core), t + 2 * (1 - core)))
    rowsf = []
    for t in range(3):
        m, c = place(t, core)
        k = lead_tile(m, c)
        c_ref[blk(m + 1), blk(c)] = k
        c_ref[blk(c + 1), blk(m)] = k.T
        for s, (a, b) in enumerate(((m, c), (c, m))):
            w = swap(2 + 2 * t + s, a, b)
            w.start()
            swaps.append(w)
        a, b = place(t, 1 - core)
        theirs += [(2 + 2 * t, a, b), (3 + 2 * t, b, a)]
        if t == 0:
            for d in range(G - 1):
                at = rows_ref.at[piece(2 * lax.rem(p - d - 1 + G, G) + core), :]
                arrived(at, r_row.at[d])
                w = copy(at, at, s_rowf.at[d], r_rowf.at[d], sibling)
                w.start()
                rowsf.append(w)
    own_rows.wait()
    own_cols.wait()

    @pl.when(p != 0)
    def _():
        own_piece.wait()
    for c in swaps:
        c.wait_send()
    for d in range(G - 1):
        arrived(rows_ref.at[piece(2 * lax.rem(p - d - 1 + G, G) + 1 - core), :], r_rowf.at[d])
        sender = lax.rem(p - d - 1 + G, G)

        @pl.when(sender != 0)
        def _():
            arrived(cols_ref.at[piece(sender), :], r_col.at[d])
    for k, m, c in theirs:
        arrived(c_ref.at[blk(m + 1), blk(c)], r_tile.at[k])

    c_ref[:256, :] = jnp.zeros((256, n), f32)
    bh[...] = jnp.zeros_like(bh)
    bl[...] = jnp.zeros_like(bl)
    kch[:64, :] = jnp.zeros((64, n), bf16)
    kcl[:64, :] = jnp.zeros((64, n), bf16)
    ri = lax.broadcasted_iota(jnp.int32, (256, 256), 0)
    ci = lax.broadcasted_iota(jnp.int32, (256, 256), 1)
    eye = jnp.where(ri == ci, 1.0, 0.0).astype(f32)
    for c in range(cols_ref.shape[0] // 256):
        roll_into(cols_ref, c * 256, r4c)
        aux[n + c * 256:n + c * 256 + 256, :] = right_lanes(cols_ref, c * 256)
    dref[...] = c_ref[256:512, :256]

    def cs(k):
        return pl.ds(k * 256, 256)

    def k_tile(t, left_ref, lo, rolled, ro, auxo, store):
        lhs = left_ref[lo, :F]
        wide = lhs.shape[0]
        for r in range(4):
            for h in range(4):
                x = rolled[r, ro, :]
                w = jnp.concatenate([x[:, 128 * ((k - h) % 4):128 * ((k - h) % 4) + 128] for k in range(4)], axis=1)
                e = jnp.exp2(dot(lhs, w, NT) * SCALE)
                if r + h == 0:
                    acc[t, :wide, :] = e
                else:
                    acc[t, :wide, :] = acc[t, :wide, :] + e
                yield
        lane = lax.broadcasted_iota(jnp.int32, (wide, 128), 1)
        left = jnp.where(lane < 64, left_ref[lo, F:].astype(f32), 0.0).astype(bf16)
        store(acc[t, :wide, :] * jnp.exp2(dot(left, aux[auxo, :], NT)))
        yield

    def solve_row(g, prev):
        x = (bh[...], bl[...])
        for c in range(4):
            r = jnp.where(jnp.int32(c) == g - 1, eye, c_ref[blk(g), cs(c)])
            xh[blk(g), cs(c)], xl[blk(g), cs(c)] = split(dot3(x, split(r), NN))
            yield

    def update(g, prev):
        for r in range(3):
            i = lax.rem(g + r, 4)
            keep = jnp.where(r < 4 - g, 1.0, 0.0).astype(f32)
            f = split(dot3(split(c_ref[blk(i + 1), blk(prev)] * keep), (bh[...], bl[...]), NT))
            yield
            for c in range(4):
                old = jnp.where(jnp.int32(c) == g - 1, 0.0, c_ref[blk(i + 1), cs(c)])
                c_ref[blk(i + 1), cs(c)] = old - dot3(f, (xh[blk(g), cs(c)], xl[blk(g), cs(c)]), NN)
                yield

    def outer(g, _):
        prev = jnp.maximum(g - 1, 0)
        nxt = jnp.minimum(g + 1, 3)

        def work():
            yield from solve_row(g, prev)
            yield from update(g, prev)
            for m in range(2):
                o = blk(2 * core + m)

                def store(k, m=m, o=o):
                    i = ri + (2 * core + m) * 256
                    k = k + jnp.where((i < 128) & (i + p * 128 == ci + g * 256), RIDGE, 0.0)
                    krh[o, blk(g)], krl[o, blk(g)] = split(k)

                yield from k_tile(m % 2, rows_ref, o, r4, blk(g), blk(g), store)
            for m in range(2):
                o = pl.ds(64 + 224 * m, 224)

                def store(k, o=o):
                    kch[o, blk(g)], kcl[o, blk(g)] = split(k)

                yield from k_tile(m % 2, cols_ref, o, r4, blk(g), blk(g), store)
            for c in range(2):
                def store(k, c=c):
                    i, j = ri + g * 256, ci + c * 256
                    same = ((i >> 7) == (j >> 6)) & (p * 128 + (i & 127) == q * 64 + (j & 63))
                    k = k + jnp.where(same, RIDGE, 0.0)
                    ktr[blk(g), cs(c)] = jnp.where(j < 64, 0.0, k)

                yield from k_tile(c % 2, rows_ref, blk(g), r4c, cs(c), cs(4 + c), store)

        todo = work()
        credit = [0.0]

        def fill(amount):
            credit[0] += amount
            while credit[0] >= 1.0:
                credit[0] -= 1.0
                next(todo, None)

        per = 114.0 / 128.0
        d00 = dref[:128, :128]
        d10 = dref[128:, :128]
        d11 = dref[128:, 128:]
        out0, out1 = [], []
        for _s in factor_steps(d00, out0):
            fill(per)
        x0 = jnp.concatenate(out0, axis=0)
        x0s = split(x0)
        l10 = split(dot3(split(d10), x0s, NT))
        fill(2)
        d11 = d11 - dot3(l10, l10, NT)
        fill(2)
        g10 = split(dot3(l10, x0s, NN))
        for _s in factor_steps(d11, out1):
            fill(per)
        for _s in todo:
            pass
        x1 = jnp.concatenate(out1, axis=0)
        x10 = -dot3(split(x1), g10, NN)
        bh[:128, :128], bl[:128, :128] = x0s
        bh[128:, :128], bl[128:, :128] = split(x10)
        bh[128:, 128:], bl[128:, 128:] = split(x1)
        f = split(dot3(split(c_ref[blk(nxt + 1), blk(g)]), (bh[...], bl[...]), NT))
        dref[...] = c_ref[blk(nxt + 1), blk(nxt)] - dot3(f, f, NT)
        for c in halves(g, core):
            c.start()
        return 0

    def halves(g, side):
        refs = [(krh, 0), (krl, 1), (krh, 2), (krl, 3)]
        return [copy(ref.at[blk(2 * side + k // 2), blk(g)], ref.at[blk(2 * side + k // 2), blk(g)],
                     s_half.at[4 * g + k], r_half.at[4 * g + k], sibling) for ref, k in refs]

    lax.fori_loop(0, 4, outer, 0)
    for _s in solve_row(4, 3):
        pass

    def pcols(m, _):
        o = pl.ds(pl.multiple_of(m * 256, 256), 256)
        for j in range(0, n, 256):
            w = j + 256
            a = dot3((kch[o, :w], kcl[o, :w]), (xh[j + 256:w + 256, :w], xl[j + 256:w + 256, :w]), NT)
            ph[o, j:w], plo[o, j:w] = split(a)
        for j in range(0, n, 256):
            w = j + 256
            a = dot3((ph[o, j:], plo[o, j:]), (xh[j + 256:, j:w], xl[j + 256:, j:w]), NN)
            zh[o, j:w], zl[o, j:w] = split(a)
        return 0

    lax.fori_loop(0, cols_ref.shape[0] // 256, pcols, 0)
    lead_rows = pl.ds(pl.multiple_of(q * 64 + 256, 64), 64)
    keep = lax.broadcasted_iota(jnp.int32, (64, n), 1) <= q * 64 + lax.broadcasted_iota(jnp.int32, (64, n), 0)
    zh[:64, :] = jnp.where(keep, -xh[lead_rows, :].astype(f32), 0.0).astype(bf16)
    zl[:64, :] = jnp.where(keep, -xl[lead_rows, :].astype(f32), 0.0).astype(bf16)

    for g in range(4):
        for c in halves(g, core):
            c.wait_send()
        for c in halves(g, 1 - core):
            c.wait_recv()
    for c in leads + passed + half + rowsf + cols:
        c.wait_send()

    def last(m, _):
        o = pl.ds(pl.multiple_of(m * 256, 256), 256)
        out[o, :] = ktr[o, :] - dot3((krh[o, :], krl[o, :]), (zh[...], zl[...]), NT)
        return 0

    lax.fori_loop(0, rows_ref.shape[0] // 256, last, 0)


def fused(pool, ids, rot):
    n = pool.shape[0]
    c = n // 2
    dma = pltpu.SemaphoreType.DMA
    v = pltpu.VMEM
    return pl.pallas_call(
        fused_kernel,
        out_shape=jax.ShapeDtypeStruct((n, c), f32),
        in_specs=[VMEM] * 4,
        out_specs=VMEM,
        scratch_shapes=[
            v((n, E), bf16), v((c, E), bf16), v((4, n, F), bf16), v((n + c, 128), bf16), v((n, E), bf16), v((n, E), bf16),
            v((n + 256, n), f32), v((n + 256, n), bf16), v((n + 256, n), bf16), v((256, 256), bf16), v((256, 256), bf16),
            v((256, 256), f32), v((4, c, F), bf16), v((n, n), bf16), v((n, n), bf16), v((c, n), bf16), v((c, n), bf16),
            v((n, c), f32), v((2, 256, 256), f32), v((c, n), bf16), v((c, n), bf16), v((c, n), bf16), v((c, n), bf16),
            dma((3,)), dma((G - 1,)), dma((1,)), dma((G - 1,)), dma((8,)), dma((7,)), dma((7,)), dma((8,)), dma((G - 1,)),
            dma((G - 1,)), dma((G - 1,)), dma((G - 1,)), dma((8,)), dma((8,)), dma((16,)), dma((16,)),
        ],
        compiler_params=pltpu.CompilerParams(collective_id=0, has_side_effects=True, vmem_limit_bytes=ROOM),
    )(pool, ids.reshape(n // 128, 128), rot.reshape(n // 128, 128), jnp.asarray(bin_table()))


def solution(mesh):
    return jax.shard_map(
        fused,
        mesh=mesh,
        in_specs=(P("row", None), P("row", None), P("row")),
        out_specs=P("row", "col"),
        check_vma=False,
    )
```
